32 devices in a mesh: grp: 2 (over y), bx: 4 (over z), by: 4 (over x, core).
Axes of the slice: x: 2, y: 2, z: 4, core: 2. Of those that a mesh axis runs over, the one named last changes fastest.
Arguments:
- psi: float32 [121, 4, 4, 256], P(None, 'bx', 'by', 'grp'), parts along dimension 3
- nbr_block: int32 [4, 4, 32, 256], P('bx', 'by', None, 'grp'), parts along dimension 3, may hold values from 0 to 8, as said below
- nbr_sphere: int32 [4, 4, 32, 256], P('bx', 'by', None, 'grp'), parts along dimension 3, may hold values from 0 to 127
- counts: int32 [4, 4, 256], P('bx', 'by', 'grp'), parts along dimension 2, may hold values from 1 to 32, as said below
- couple: bfloat16 [302, 4, 4, 32, 256], P(None, 'bx', 'by', None, 'grp'), parts along dimension 4, may hold values from 0.135 to 0.25
- ratio: float32 [4, 4, 32, 256], P('bx', 'by', None, 'grp'), parts along dimension 3, may hold values from 0.75 to 0.85
Outputs:
- solution: float32 [121, 4, 4, 256], P(None, 'bx', 'by', 'grp'), parts along dimension 3
- step_norms: float32 [6], P('grp'), parts along dimension 0
The draws below stay inside these ranges and needn't reach their ends.
There are 2 independent parts, one for each index of `grp`. The reference program is written for one: setup_inputs(seed, part) draws one part's arguments, and reference() takes and returns one part's arrays. A program takes and returns all parts, laid end to end along the dimension named above; each array names one. Nothing has to cross between parts.
Inputs may be any that keep to these rules, and one draw needn't show every extreme that they name: `nbr_block`: every named block lies inside the grid of blocks. `counts`: in every block some sphere uses the block's largest count, which lies between 16 and 32; in some block it is all 32.
All inputs are finite; a program needn't handle non-finite values.
Results may differ from the reference program's by a relative error of at most 0.0003.
Values sent between devices are 32-bit elements; how exact they have to be, the bound alone decides.
A program may use at most 64 MiB of HBM per device.

```python
import math
import jax
import jax.numpy as jnp
import numpy as np
from jax import lax

LMAX = 10
LH = 121
NG = 302
SLOTS = 32
SWEEPS = 3
SPH = 128
BLOCKS_X = 4
BLOCKS_Y = 4


def draw_psi(key, part):
    key = jax.random.fold_in(key, 11)
    first = jax.random.fold_in(key, 0)
    ramp = 0.6 + 1.2 * jnp.arange(BLOCKS_X, dtype=jnp.float32) / (BLOCKS_X - 1)
    shape = (LH, BLOCKS_X, BLOCKS_Y, SPH)
    values = jnp.clip(jax.random.normal(first, shape, jnp.float32), -6.0, 6.0)
    return values * ramp[None, :, None, None]


def draw_nbr_block(key, part):
    key = jax.random.fold_in(key, 23)
    shape = (BLOCKS_X, BLOCKS_Y, SLOTS, SPH)
    code = jax.random.randint(key, shape, 0, 40)
    other = jnp.mod(code + 7, 8)
    other = other + (other >= 4).astype(jnp.int32)
    direction = jnp.where(code == 0, 4, other).astype(jnp.int32)
    step_x = direction // 3 - 1
    step_y = direction % 3 - 1
    pos_x = jnp.arange(BLOCKS_X, dtype=jnp.int32)[:, None, None, None]
    pos_y = jnp.arange(BLOCKS_Y, dtype=jnp.int32)[None, :, None, None]
    step_x = jnp.where((pos_x == 0) & (step_x < 0), 1, step_x)
    step_x = jnp.where((pos_x == BLOCKS_X - 1) & (step_x > 0), -1, step_x)
    step_y = jnp.where((pos_y == 0) & (step_y < 0), 1, step_y)
    step_y = jnp.where((pos_y == BLOCKS_Y - 1) & (step_y > 0), -1, step_y)
    return ((step_x + 1) * 3 + (step_y + 1)).astype(jnp.int32)


def draw_counts(key, part):
    key = jax.random.fold_in(key, 37)
    first, second, third = jax.random.split(key, 3)
    caps = jax.random.randint(first, (BLOCKS_X * BLOCKS_Y,), SLOTS // 2, SLOTS + 1)
    chosen = jax.random.randint(second, (), 0, BLOCKS_X * BLOCKS_Y)
    caps = jnp.where(jnp.arange(BLOCKS_X * BLOCKS_Y) == chosen, SLOTS, caps).reshape(BLOCKS_X, BLOCKS_Y, 1)
    values = jax.random.randint(third, (BLOCKS_X, BLOCKS_Y, SPH), 0, 1 << 20) % caps + 1
    values = jnp.where(jnp.arange(SPH)[None, None, :] == 0, caps, values)
    return values.astype(jnp.int32)


def draw_couple(key, part):
    key = jax.random.fold_in(key, 53)
    first, second = jax.random.split(key)
    level = jax.random.uniform(first, (1, BLOCKS_X, BLOCKS_Y, SLOTS, SPH), jnp.float32, 0.16, 0.22)
    factor = jax.random.uniform(second, (NG, BLOCKS_X, BLOCKS_Y, SLOTS, SPH), jnp.float32, 0.85, 1.13)
    return (level * factor).astype(jnp.bfloat16)


def with_ends(result, rng, smallest, high):
    spot = [jax.random.randint(jax.random.fold_in(rng, axis), (), 0, length) for axis, length in enumerate(result.shape)]
    longest = result.shape.index(max(result.shape))
    beside = spot[:longest] + [(spot[longest] + 1) % result.shape[longest]] + spot[longest + 1:]
    return result.at[tuple(spot)].set(smallest).at[tuple(beside)].set(high)


def level_of(key, dims, cuts, low, high):
    level, own = 1.0, jax.random.fold_in(key, 6)
    for axis_at, blocks in cuts:
        heights = jnp.exp(jax.random.uniform(jax.random.fold_in(own, axis_at), (blocks,), jnp.float32, low / len(cuts), high / len(cuts)))
        level = level * jnp.repeat(heights, dims[axis_at] // blocks).reshape([-1 if axis == axis_at else 1 for axis in range(len(dims))])
    return level


def setup_inputs(seed: int = 0, part: int = 0) -> dict:
    keys = jax.random.split(jax.random.key(seed), 7)
    own_keys = jax.random.split(jax.random.fold_in(keys[6], part), 7)
    return {
        "psi": draw_psi(jax.random.fold_in(jax.random.fold_in(keys[6], part), 71), part),
        "nbr_block": draw_nbr_block(jax.random.fold_in(jax.random.fold_in(keys[6], part), 71), part),
        "nbr_sphere": with_ends(jax.random.randint(own_keys[2], (BLOCKS_X, BLOCKS_Y, SLOTS, SPH), 0, SPH), jax.random.fold_in(own_keys[2], 1), 0, SPH - 1).astype(jnp.int32),
        "counts": draw_counts(jax.random.fold_in(jax.random.fold_in(keys[6], part), 71), part),
        "couple": draw_couple(jax.random.fold_in(jax.random.fold_in(keys[6], part), 71), part),
        "ratio": jnp.clip(0.75 + 0.100000024 * jax.random.uniform(own_keys[5], (BLOCKS_X, BLOCKS_Y, SLOTS, SPH), jnp.float32) ** level_of(own_keys[5], (BLOCKS_X, BLOCKS_Y, SLOTS, SPH), ((0, 4), (1, 4)), -0.2, 0.2), 0.75, 0.85),
    }


golden = 2.399963229728653

def basis_table(npts, lmax):
    index = jnp.arange(npts, dtype=jnp.float32)
    zval = 1.0 - (2.0 * index + 1.0) / npts
    sinval = jnp.sqrt(jnp.maximum(1.0 - zval * zval, 0.0))
    angle = golden * index
    table = {(0, 0): jnp.full((npts,), 1.0 / math.sqrt(4.0 * math.pi), jnp.float32)}
    for order in range(1, lmax + 1):
        table[order, order] = -math.sqrt((2.0 * order + 1.0) / (2.0 * order)) * sinval * table[order - 1, order - 1]
    for order in range(0, lmax):
        table[order + 1, order] = math.sqrt(2.0 * order + 3.0) * zval * table[order, order]
    for order in range(0, lmax + 1):
        for degree in range(order + 2, lmax + 1):
            first = math.sqrt((4.0 * degree * degree - 1.0) / (degree * degree - order * order))
            second = math.sqrt(((degree - 1.0) ** 2 - order * order) / (4.0 * (degree - 1.0) ** 2 - 1.0))
            table[degree, order] = first * (zval * table[degree - 1, order] - second * table[degree - 2, order])
    columns = []
    for degree in range(lmax + 1):
        for order in range(-degree, degree + 1):
            if order < 0:
                columns.append(math.sqrt(2.0) * table[degree, -order] * jnp.sin(-order * angle))
            elif order == 0:
                columns.append(table[degree, 0])
            else:
                columns.append(math.sqrt(2.0) * table[degree, order] * jnp.cos(order * angle))
    return jnp.stack(columns, axis=1)

def degree_list(lmax):
    return np.repeat(np.arange(lmax + 1), 2 * np.arange(lmax + 1) + 1).astype(np.float32)

def coupled_terms(basis, points, index, couple_part, ratio_part, mask_part, degrees):
    npts = basis.shape[0]
    taken = jnp.take(points, index.reshape(-1), axis=1)
    product = taken * couple_part.reshape(npts, -1).astype(jnp.float32)
    back = lax.dot_general(basis, product, (((0,), (0,)), ((), ())), precision=lax.Precision.HIGHEST, preferred_element_type=jnp.float32)
    back = back.reshape(basis.shape[1], index.shape[0], index.shape[1])
    power = ratio_part[None] ** jnp.asarray(degrees)[:, None, None]
    return lax.optimization_barrier(jnp.sum(jnp.where(mask_part[None], back * power, 0.0), axis=1))

def reference(psi, nbr_block, nbr_sphere, counts, couple, ratio):
    basis = basis_table(NG, LMAX)
    degrees = degree_list(LMAX)
    quad = 4.0 * math.pi / NG
    dcoef = jnp.asarray(4.0 * math.pi / (2.0 * degrees + 1.0))[:, None, None, None]
    solution = psi / dcoef
    changes = []
    for sweep in range(SWEEPS):
        padded = jnp.pad(solution, ((0, 0), (1, 1), (1, 1), (0, 0)))

        def one_block(flat):
            row = flat // BLOCKS_Y
            col = flat % BLOCKS_Y
            zero = jnp.zeros((), jnp.int32)
            rim = lax.dynamic_slice(padded, (zero, row, col, zero), (LH, 3, 3, SPH))
            points = quad * jnp.dot(basis, rim.reshape(LH, 9 * SPH), precision=lax.Precision.HIGHEST, preferred_element_type=jnp.float32)
            index = nbr_block[row, col] * SPH + nbr_sphere[row, col]
            mask = jnp.arange(SLOTS, dtype=jnp.int32)[:, None] < counts[row, col][None, :]
            return coupled_terms(basis, points, index, couple[:, row, col], ratio[row, col], mask, degrees)
        blocks = lax.map(one_block, jnp.arange(BLOCKS_X * BLOCKS_Y, dtype=jnp.int32))
        coupled = jnp.transpose(blocks.reshape(BLOCKS_X, BLOCKS_Y, LH, SPH), (2, 0, 1, 3))
        fresh = (psi - coupled) / dcoef
        changes.append(jnp.sum((fresh - solution) ** 2))
        solution = fresh
    total = jnp.stack(changes)
    return (solution, jnp.sqrt(total / (LH * BLOCKS_X * BLOCKS_Y * SPH)))
```

```python
import functools
import math

import jax
import jax.numpy as jnp
import numpy as np
from jax import lax
from jax.experimental import pallas as pl
from jax.experimental.pallas import tpu as pltpu
from jax.sharding import PartitionSpec as P

SWEEPS = 3
MESH = pl.DeviceIdType.MESH
GOLDEN = 2.399963229728653
HP = 128
WIDE = 2
BF = jnp.bfloat16
F32 = jnp.float32


def basis_table(npts, lmax):
    index = np.arange(npts, dtype=np.float64)
    zval = 1.0 - (2.0 * index + 1.0) / npts
    sinval = np.sqrt(np.maximum(1.0 - zval * zval, 0.0))
    angle = GOLDEN * index
    table = {(0, 0): np.full((npts,), 1.0 / math.sqrt(4.0 * math.pi))}
    for order in range(1, lmax + 1):
        table[order, order] = (
            -math.sqrt((2.0 * order + 1.0) / (2.0 * order)) * sinval * table[order - 1, order - 1]
        )
    for order in range(0, lmax):
        table[order + 1, order] = math.sqrt(2.0 * order + 3.0) * zval * table[order, order]
    for order in range(0, lmax + 1):
        for degree in range(order + 2, lmax + 1):
            first = math.sqrt((4.0 * degree * degree - 1.0) / (degree * degree - order * order))
            second = math.sqrt(
                ((degree - 1.0) ** 2 - order * order) / (4.0 * (degree - 1.0) ** 2 - 1.0)
            )
            table[degree, order] = first * (
                zval * table[degree - 1, order] - second * table[degree - 2, order]
            )
    columns = []
    for degree in range(lmax + 1):
        for order in range(-degree, degree + 1):
            if order < 0:
                columns.append(math.sqrt(2.0) * table[degree, -order] * np.sin(-order * angle))
            elif order == 0:
                columns.append(table[degree, 0])
            else:
                columns.append(math.sqrt(2.0) * table[degree, order] * np.cos(order * angle))
    return np.stack(columns, axis=1)


def split_np(x):
    hi = x.astype(np.float32).astype(BF)
    lo = (x - hi.astype(np.float64)).astype(np.float32).astype(BF)
    return hi, lo


def kernel(
    nbx, nby, cells,
    psi_ref, nblk_ref, nsph_ref, cnt_ref, couple_ref, ratio_ref, bc_ref, bt_ref, deg_ref, invd_ref,
    out_ref, norm_ref,
    cin, cf, cd, onehot, power, land, solcat, sol0, nb, nland1, nland2,
    csem, ssem, rsem, s1, r1, s2, r2,
):
    lh, sph = psi_ref.shape
    npts, slots, _ = couple_ref.shape
    npad = bc_ref.shape[0]
    groups = slots // WIDE
    wide = WIDE * sph
    ix, iy, ig = lax.axis_index("bx"), lax.axis_index("by"), lax.axis_index("grp")

    copy_in = pltpu.make_async_copy(couple_ref, cin, csem)
    copy_in.start()

    dirs = [d for d in range(9) if d != 4]
    inside = {}
    for d in dirs:
        tx, ty = ix + d // 3 - 1, iy + d % 3 - 1
        inside[d] = (tx >= 0) & (tx < nbx) & (ty >= 0) & (ty < nby)

    def device(d):
        return (ig, ix + d // 3 - 1, iy + d % 3 - 1)

    barrier = pltpu.get_barrier_semaphore()
    count = jnp.int32(0)
    for d in dirs:
        count = count + inside[d].astype(jnp.int32)

        @pl.when(inside[d])
        def _(d=d):
            pl.semaphore_signal(barrier, inc=1, device_id=device(d), device_id_type=MESH)

    for off in range(1, nby):
        peer = lax.rem(iy + off, nby)
        far = jnp.abs(peer - iy) >= 2
        count = count + far.astype(jnp.int32)

        @pl.when(far)
        def _(peer=peer):
            pl.semaphore_signal(barrier, inc=1, device_id=(ig, ix, peer), device_id_type=MESH)

    for off in range(1, nbx):
        peer = lax.rem(ix + off, nbx)
        far = jnp.abs(peer - ix) >= 2
        count = count + far.astype(jnp.int32)

        @pl.when(far)
        def _(peer=peer):
            pl.semaphore_signal(barrier, inc=1, device_id=(ig, peer, iy), device_id_type=MESH)

    sol0[...] = jnp.zeros_like(sol0)
    sol0[pl.ds(0, lh), :] = psi_ref[...] * invd_ref[pl.ds(0, lh), :]
    land[0, 4] = sol0[...]
    pl.semaphore_wait(barrier, count)

    def block_copy(t, d):
        return pltpu.make_async_remote_copy(
            src_ref=land.at[t, 4],
            dst_ref=land.at[t, 8 - d],
            send_sem=ssem.at[t, d],
            recv_sem=rsem.at[t, 8 - d],
            device_id=device(d),
            device_id_type=MESH,
        )

    def block_arrival(t, d):
        return pltpu.make_async_remote_copy(
            src_ref=land.at[t, 4],
            dst_ref=land.at[t, d],
            send_sem=ssem.at[t, d],
            recv_sem=rsem.at[t, d],
            device_id=device(d),
            device_id_type=MESH,
        )

    def send_all(t):
        for d in dirs:
            @pl.when(inside[d])
            def _(d=d):
                block_copy(t, d).start()

    def place(block, d):
        hi = block.astype(BF)
        lo = (block - hi.astype(F32)).astype(BF)
        solcat[pl.ds(0, HP), pl.ds(d * sph, sph)] = hi
        solcat[pl.ds(HP, HP), pl.ds(d * sph, sph)] = lo

    send_all(0)

    rows = lax.broadcasted_iota(jnp.int32, (9 * sph, sph), 0)

    def prepare(g, carry):
        for w in range(WIDE):
            s = g * WIDE + w
            lanes = pl.ds(w * sph, sph)
            index = nblk_ref[pl.ds(s, 1), :] * sph + nsph_ref[pl.ds(s, 1), :]
            onehot[g, :, lanes] = (rows == index).astype(F32).astype(BF)
            logr = jnp.log(ratio_ref[pl.ds(s, 1), :])
            raised = jnp.exp(deg_ref[...] * logr) * invd_ref[...]
            power[g, :, lanes] = jnp.where(s < cnt_ref[...], raised, 0.0)
        return carry

    lax.fori_loop(0, groups, prepare, 0)

    copy_in.wait()

    def widen(n, carry):
        cf[pl.ds(n * slots, slots), :] = cin[n].astype(F32)
        return carry

    lax.fori_loop(0, npts, widen, 0, unroll=2)
    cf[pl.ds(npts * slots, (npad - npts) * slots), :] = jnp.zeros(((npad - npts) * slots, sph), F32)

    def turn(g, carry):
        for w in range(WIDE):
            cd[g, :, pl.ds(w * sph, sph)] = cf[pl.ds(g * WIDE + w, npad, stride=slots), :]
        return carry

    lax.fori_loop(0, groups, turn, 0)

    nb[...] = jnp.zeros_like(nb)
    for t in range(SWEEPS):
        old = land[t, 4]
        place(old, 4)
        for d in dirs:
            @pl.when(inside[d])
            def _(d=d, t=t):
                block_arrival(t, d).wait_recv()
                place(land[t, d], d)

            if t == 0:
                @pl.when(jnp.logical_not(inside[d]))
                def _(d=d):
                    solcat[:, pl.ds(d * sph, sph)] = jnp.zeros((2 * HP, sph), BF)

        def pairs(g, total):
            picked = jnp.dot(solcat[...], onehot[g], preferred_element_type=F32).astype(BF)
            stacked = jnp.concatenate([picked, picked[:HP]], axis=0)
            points = jnp.dot(bc_ref[...], stacked, preferred_element_type=F32)
            product = points * cd[g]
            hi = product.astype(BF)
            lo = (product - hi.astype(F32)).astype(BF)
            back = jnp.dot(
                bt_ref[...], jnp.concatenate([hi, lo, hi], axis=0), preferred_element_type=F32
            )
            terms = back * power[g]
            for w in range(WIDE):
                total = total + terms[:, w * sph:(w + 1) * sph]
            return total

        total = lax.fori_loop(0, groups, pairs, jnp.zeros((HP, sph), F32), unroll=2)
        fresh = sol0[...] - total
        if t < SWEEPS - 1:
            land[t + 1, 4] = fresh
            send_all(t + 1)
        else:
            out_ref[...] = fresh[:lh]
        nb[pl.ds(t, 1), :] = jnp.sum((fresh - old) ** 2, axis=0, keepdims=True)

    def reduce_line(mine, slots_ref, send, recv, me, count, where):
        slots_ref[me] = mine
        copies = []
        for off in range(1, count):
            peer = lax.rem(me + off, count)
            copy = pltpu.make_async_remote_copy(
                src_ref=slots_ref.at[me],
                dst_ref=slots_ref.at[me],
                send_sem=send.at[off],
                recv_sem=recv.at[me],
                device_id=where(peer),
                device_id_type=MESH,
            )
            copy.start()
            copies.append(copy)
        for off in range(1, count):
            peer = lax.rem(me + off, count)
            pltpu.make_async_remote_copy(
                src_ref=slots_ref.at[me],
                dst_ref=slots_ref.at[peer],
                send_sem=send.at[off],
                recv_sem=recv.at[peer],
                device_id=where(peer),
                device_id_type=MESH,
            ).wait_recv()
        result = slots_ref[0]
        for i in range(1, count):
            result = result + slots_ref[i]
        for copy in copies:
            copy.wait_send()
        return result

    part = reduce_line(nb[...], nland1, s1, r1, iy, nby, lambda p: (ig, ix, p))
    part = reduce_line(part, nland2, s2, r2, ix, nbx, lambda p: (ig, p, iy))
    norm = jnp.sqrt(jnp.sum(part, axis=1, keepdims=True) * (1.0 / cells))
    norm_ref[...] = jnp.broadcast_to(norm, norm_ref.shape)

    for t in range(SWEEPS):
        for d in dirs:
            @pl.when(inside[d])
            def _(d=d, t=t):
                block_copy(t, d).wait_send()


def on_device(nbx, nby, psi, nbr_block, nbr_sphere, counts, couple, ratio):
    lh, sph = psi.shape[0], psi.shape[3]
    slots = nbr_block.shape[2]
    npts = couple.shape[0]
    lmax = math.isqrt(lh) - 1
    npad = -(-npts // 16) * 16
    basis = np.zeros((npad, HP))
    basis[:npts, :lh] = basis_table(npts, lmax)
    degrees = np.zeros((HP,))
    degrees[:lh] = np.repeat(np.arange(lmax + 1), 2 * np.arange(lmax + 1) + 1)
    inverse = (2.0 * degrees + 1.0) / (4.0 * math.pi)
    inverse[lh:] = 0.0
    hi, lo = split_np(basis * (4.0 * math.pi / npts))
    bc = np.concatenate([hi, hi, lo], axis=1)
    hi, lo = split_np(basis.T)
    bt = np.concatenate([hi, hi, lo], axis=1)
    deg = np.broadcast_to(degrees[:, None], (HP, sph)).astype(np.float32)
    invd = np.broadcast_to(inverse[:, None], (HP, sph)).astype(np.float32)
    cells = lh * sph * nbx * nby
    groups = slots // WIDE
    vmem = pl.BlockSpec(memory_space=pltpu.VMEM)
    out, norms = pl.pallas_call(
        functools.partial(kernel, nbx, nby, cells),
        out_shape=(
            jax.ShapeDtypeStruct((lh, sph), F32),
            jax.ShapeDtypeStruct((8, 128), F32),
        ),
        in_specs=[vmem] * 4 + [pl.BlockSpec(memory_space=pl.ANY)] + [vmem] * 5,
        out_specs=(vmem, vmem),
        scratch_shapes=[
            pltpu.VMEM((npts, slots, sph), BF),
            pltpu.VMEM((npad * slots, sph), F32),
            pltpu.VMEM((groups, npad, WIDE * sph), F32),
            pltpu.VMEM((groups, 9 * sph, WIDE * sph), BF),
            pltpu.VMEM((groups, HP, WIDE * sph), F32),
            pltpu.VMEM((SWEEPS, 9, HP, sph), F32),
            pltpu.VMEM((2 * HP, 9 * sph), BF),
            pltpu.VMEM((HP, sph), F32),
            pltpu.VMEM((8, sph), F32),
            pltpu.VMEM((nby, 8, sph), F32),
            pltpu.VMEM((nbx, 8, sph), F32),
            pltpu.SemaphoreType.DMA(()),
            pltpu.SemaphoreType.DMA((SWEEPS, 9)),
            pltpu.SemaphoreType.DMA((SWEEPS, 9)),
            pltpu.SemaphoreType.DMA((nby,)),
            pltpu.SemaphoreType.DMA((nby,)),
            pltpu.SemaphoreType.DMA((nbx,)),
            pltpu.SemaphoreType.DMA((nbx,)),
        ],
        compiler_params=pltpu.CompilerParams(
            collective_id=0, has_side_effects=True, vmem_limit_bytes=48 * 1024 * 1024
        ),
        cost_estimate=pl.CostEstimate(
            flops=2 * SWEEPS * slots * sph * (2304 * HP + 6 * npad * HP),
            bytes_accessed=4 * 1024 * 1024,
            transcendentals=slots * sph * HP,
        ),
    )(
        psi.reshape(lh, sph),
        nbr_block.reshape(slots, sph),
        nbr_sphere.reshape(slots, sph),
        counts.reshape(1, sph),
        couple.reshape(npts, slots, sph),
        ratio.reshape(slots, sph),
        jnp.asarray(bc),
        jnp.asarray(bt),
        jnp.asarray(deg),
        jnp.asarray(invd),
    )
    return out.reshape(lh, 1, 1, sph), norms[:SWEEPS, 0]


def solution(mesh):
    return jax.shard_map(
        functools.partial(on_device, mesh.shape["bx"], mesh.shape["by"]),
        mesh=mesh,
        in_specs=(
            P(None, "bx", "by", "grp"),
            P("bx", "by", None, "grp"),
            P("bx", "by", None, "grp"),
            P("bx", "by", "grp"),
            P(None, "bx", "by", None, "grp"),
            P("bx", "by", None, "grp"),
        ),
        out_specs=(P(None, "bx", "by", "grp"), P("grp")),
        check_vma=False,
    )
```

```python
import functools
import math

import jax
import jax.numpy as jnp
import numpy as np
from jax import lax
from jax.experimental import pallas as pl
from jax.experimental.pallas import tpu as pltpu
from jax.sharding import PartitionSpec as P

SWEEPS = 3
MESH = pl.DeviceIdType.MESH
GOLDEN = 2.399963229728653
HP = 128
WIDE = 8
BF = jnp.bfloat16
F32 = jnp.float32


def basis_table(npts, lmax):
    index = np.arange(npts, dtype=np.float64)
    zval = 1.0 - (2.0 * index + 1.0) / npts
    sinval = np.sqrt(np.maximum(1.0 - zval * zval, 0.0))
    angle = GOLDEN * index
    table = {(0, 0): np.full((npts,), 1.0 / math.sqrt(4.0 * math.pi))}
    for order in range(1, lmax + 1):
        table[order, order] = (
            -math.sqrt((2.0 * order + 1.0) / (2.0 * order)) * sinval * table[order - 1, order - 1]
        )
    for order in range(0, lmax):
        table[order + 1, order] = math.sqrt(2.0 * order + 3.0) * zval * table[order, order]
    for order in range(0, lmax + 1):
        for degree in range(order + 2, lmax + 1):
            first = math.sqrt((4.0 * degree * degree - 1.0) / (degree * degree - order * order))
            second = math.sqrt(
                ((degree - 1.0) ** 2 - order * order) / (4.0 * (degree - 1.0) ** 2 - 1.0)
            )
            table[degree, order] = first * (
                zval * table[degree - 1, order] - second * table[degree - 2, order]
            )
    columns = []
    for degree in range(lmax + 1):
        for order in range(-degree, degree + 1):
            if order < 0:
                columns.append(math.sqrt(2.0) * table[degree, -order] * np.sin(-order * angle))
            elif order == 0:
                columns.append(table[degree, 0])
            else:
                columns.append(math.sqrt(2.0) * table[degree, order] * np.cos(order * angle))
    return np.stack(columns, axis=1)


def kernel(
    nbx, nby, cells,
    psi_hbm, nblk_hbm, nsph_hbm, cnt_hbm, couple_hbm, ratio_hbm, basis_hbm, basist_hbm,
    out_ref, norm_ref,
    psi_ref, nblk_ref, nsph_ref, cnt_ref, cin, ratio_ref, basis_ref, basist_ref,
    bc_ref, bt_ref, cf, cd, onehot, power, land, solcat, sol0, nb, nland1, nland2,
    csem, ssem, rsem, s1, r1, s2, r2,
):
    lh, sph = psi_ref.shape
    npts, slots, _ = cin.shape
    npad = basis_ref.shape[0]
    groups = slots // WIDE
    wide = WIDE * sph
    ix, iy, ig = lax.axis_index("bx"), lax.axis_index("by"), lax.axis_index("grp")

    sources = (psi_hbm, nblk_hbm, nsph_hbm, cnt_hbm, ratio_hbm, basis_hbm, basist_hbm, couple_hbm)
    places = (psi_ref, nblk_ref, nsph_ref, cnt_ref, ratio_ref, basis_ref, basist_ref, cin)
    loads = [
        pltpu.make_async_copy(source, target, csem.at[i])
        for i, (source, target) in enumerate(zip(sources, places))
    ]
    for load in loads:
        load.start()

    dirs = [d for d in range(9) if d != 4]
    inside = {}
    for d in dirs:
        tx, ty = ix + d // 3 - 1, iy + d % 3 - 1
        inside[d] = (tx >= 0) & (tx < nbx) & (ty >= 0) & (ty < nby)

    def device(d):
        return (ig, ix + d // 3 - 1, iy + d % 3 - 1)

    barrier = pltpu.get_barrier_semaphore()
    count = jnp.int32(0)
    for d in dirs:
        count = count + inside[d].astype(jnp.int32)

        @pl.when(inside[d])
        def _(d=d):
            pl.semaphore_signal(barrier, inc=1, device_id=device(d), device_id_type=MESH)

    for off in range(1, nby):
        peer = lax.rem(iy + off, nby)
        far = jnp.abs(peer - iy) >= 2
        count = count + far.astype(jnp.int32)

        @pl.when(far)
        def _(peer=peer):
            pl.semaphore_signal(barrier, inc=1, device_id=(ig, ix, peer), device_id_type=MESH)

    for off in range(1, nbx):
        peer = lax.rem(ix + off, nbx)
        far = jnp.abs(peer - ix) >= 2
        count = count + far.astype(jnp.int32)

        @pl.when(far)
        def _(peer=peer):
            pl.semaphore_signal(barrier, inc=1, device_id=(ig, peer, iy), device_id_type=MESH)

    row = lax.broadcasted_iota(jnp.int32, (HP, sph), 0)
    degree = jnp.zeros((HP, sph), F32)
    for level in range(1, math.isqrt(lh)):
        degree = degree + (row >= level * level).astype(F32)
    inverse = jnp.where(row < lh, (2.0 * degree + 1.0) * (1.0 / (4.0 * math.pi)), 0.0)
    sol0[...] = jnp.zeros_like(sol0)
    loads[0].wait()
    sol0[pl.ds(0, lh), :] = psi_ref[...] * inverse[:lh]
    land[0, 4] = sol0[...]
    pl.semaphore_wait(barrier, count)

    def block_copy(t, d):
        return pltpu.make_async_remote_copy(
            src_ref=land.at[t, 4],
            dst_ref=land.at[t, 8 - d],
            send_sem=ssem.at[t, d],
            recv_sem=rsem.at[t, 8 - d],
            device_id=device(d),
            device_id_type=MESH,
        )

    def block_arrival(t, d):
        return pltpu.make_async_remote_copy(
            src_ref=land.at[t, 4],
            dst_ref=land.at[t, d],
            send_sem=ssem.at[t, d],
            recv_sem=rsem.at[t, d],
            device_id=device(d),
            device_id_type=MESH,
        )

    def send_all(t):
        for d in dirs:
            @pl.when(inside[d])
            def _(d=d):
                block_copy(t, d).start()

    def place(block, d):
        hi = block.astype(BF)
        lo = (block - hi.astype(F32)).astype(BF)
        solcat[pl.ds(0, HP), pl.ds(d * sph, sph)] = hi
        solcat[pl.ds(HP, HP), pl.ds(d * sph, sph)] = lo

    send_all(0)

    for load in loads[1:7]:
        load.wait()
    rows = lax.broadcasted_iota(jnp.int32, (9 * sph, sph), 0)

    def prepare(g, carry):
        for w in range(WIDE):
            s = g * WIDE + w
            lanes = pl.ds(w * sph, sph)
            index = nblk_ref[pl.ds(s, 1), :] * sph + nsph_ref[pl.ds(s, 1), :]
            onehot[g, :, lanes] = (rows == index).astype(F32).astype(BF)
            logr = jnp.log(ratio_ref[pl.ds(s, 1), :])
            raised = jnp.exp(degree * logr) * inverse
            power[g, :, lanes] = jnp.where(s < cnt_ref[...], raised, 0.0)
        return carry

    lax.fori_loop(0, groups, prepare, 0)

    quad = 4.0 * math.pi / npts
    for source, target, width, scale in (
        (basis_ref, bc_ref, HP, quad),
        (basist_ref, bt_ref, npad, 1.0),
    ):
        value = source[...] * scale
        hi = value.astype(BF)
        target[:, pl.ds(0, width)] = hi
        target[:, pl.ds(width, width)] = hi
        target[:, pl.ds(2 * width, width)] = (value - hi.astype(F32)).astype(BF)

    loads[7].wait()

    def widen(n, carry):
        cf[pl.ds(n * slots, slots), :] = cin[n].astype(F32)
        return carry

    lax.fori_loop(0, npts, widen, 0, unroll=2)
    cf[pl.ds(npts * slots, (npad - npts) * slots), :] = jnp.zeros(((npad - npts) * slots, sph), F32)

    def turn(g, carry):
        for w in range(WIDE):
            cd[g, :, pl.ds(w * sph, sph)] = cf[pl.ds(g * WIDE + w, npad, stride=slots), :]
        return carry

    lax.fori_loop(0, groups, turn, 0)

    nb[...] = jnp.zeros_like(nb)
    for t in range(SWEEPS):
        old = land[t, 4]
        place(old, 4)
        for d in dirs:
            @pl.when(inside[d])
            def _(d=d, t=t):
                block_arrival(t, d).wait_recv()
                place(land[t, d], d)

            if t == 0:
                @pl.when(jnp.logical_not(inside[d]))
                def _(d=d):
                    solcat[:, pl.ds(d * sph, sph)] = jnp.zeros((2 * HP, sph), BF)

        def pairs(g, total):
            picked = jnp.dot(solcat[...], onehot[g], preferred_element_type=F32).astype(BF)
            stacked = jnp.concatenate([picked, picked[:HP]], axis=0)
            points = jnp.dot(bc_ref[...], stacked, preferred_element_type=F32)
            product = points * cd[g]
            hi = product.astype(BF)
            lo = (product - hi.astype(F32)).astype(BF)
            back = jnp.dot(
                bt_ref[...], jnp.concatenate([hi, lo, hi], axis=0), preferred_element_type=F32
            )
            terms = back * power[g]
            for w in range(WIDE):
                total = total + terms[:, w * sph:(w + 1) * sph]
            return total

        total = lax.fori_loop(0, groups, pairs, jnp.zeros((HP, sph), F32), unroll=2)
        fresh = sol0[...] - total
        if t < SWEEPS - 1:
            land[t + 1, 4] = fresh
            send_all(t + 1)
        else:
            out_ref[...] = fresh[:lh]
        nb[pl.ds(t, 1), :] = jnp.sum((fresh - old) ** 2, axis=0, keepdims=True)

    def reduce_line(mine, slots_ref, send, recv, me, count, where):
        slots_ref[me] = mine
        copies = []
        for off in range(1, count):
            peer = lax.rem(me + off, count)
            copy = pltpu.make_async_remote_copy(
                src_ref=slots_ref.at[me],
                dst_ref=slots_ref.at[me],
                send_sem=send.at[off],
                recv_sem=recv.at[me],
                device_id=where(peer),
                device_id_type=MESH,
            )
            copy.start()
            copies.append(copy)
        for off in range(1, count):
            peer = lax.rem(me + off, count)
            pltpu.make_async_remote_copy(
                src_ref=slots_ref.at[me],
                dst_ref=slots_ref.at[peer],
                send_sem=send.at[off],
                recv_sem=recv.at[peer],
                device_id=where(peer),
                device_id_type=MESH,
            ).wait_recv()
        result = slots_ref[0]
        for i in range(1, count):
            result = result + slots_ref[i]
        for copy in copies:
            copy.wait_send()
        return result

    part = reduce_line(nb[...], nland1, s1, r1, iy, nby, lambda p: (ig, ix, p))
    part = reduce_line(part, nland2, s2, r2, ix, nbx, lambda p: (ig, p, iy))
    norm = jnp.sqrt(jnp.sum(part, axis=1, keepdims=True) * (1.0 / cells))
    norm_ref[...] = jnp.broadcast_to(norm, norm_ref.shape)

    for t in range(SWEEPS):
        for d in dirs:
            @pl.when(inside[d])
            def _(d=d, t=t):
                block_copy(t, d).wait_send()


def on_device(nbx, nby, psi, nbr_block, nbr_sphere, counts, couple, ratio):
    lh, sph = psi.shape[0], psi.shape[3]
    slots = nbr_block.shape[2]
    npts = couple.shape[0]
    lmax = math.isqrt(lh) - 1
    npad = -(-npts // 16) * 16
    basis = np.zeros((npad, HP))
    basis[:npts, :lh] = basis_table(npts, lmax)
    cells = lh * sph * nbx * nby
    groups = slots // WIDE
    vmem = pl.BlockSpec(memory_space=pltpu.VMEM)
    out, norms = pl.pallas_call(
        functools.partial(kernel, nbx, nby, cells),
        out_shape=(
            jax.ShapeDtypeStruct((lh, sph), F32),
            jax.ShapeDtypeStruct((8, 128), F32),
        ),
        in_specs=[pl.BlockSpec(memory_space=pltpu.HBM)] * 8,
        out_specs=(vmem, vmem),
        scratch_shapes=[
            pltpu.VMEM((lh, sph), F32),
            pltpu.VMEM((slots, sph), jnp.int32),
            pltpu.VMEM((slots, sph), jnp.int32),
            pltpu.VMEM((1, sph), jnp.int32),
            pltpu.VMEM((npts, slots, sph), BF),
            pltpu.VMEM((slots, sph), F32),
            pltpu.VMEM((npad, HP), F32),
            pltpu.VMEM((HP, npad), F32),
            pltpu.VMEM((npad, 3 * HP), BF),
            pltpu.VMEM((HP, 3 * npad), BF),
            pltpu.VMEM((npad * slots, sph), F32),
            pltpu.VMEM((groups, npad, WIDE * sph), F32),
            pltpu.VMEM((groups, 9 * sph, WIDE * sph), BF),
            pltpu.VMEM((groups, HP, WIDE * sph), F32),
            pltpu.VMEM((SWEEPS, 9, HP, sph), F32),
            pltpu.VMEM((2 * HP, 9 * sph), BF),
            pltpu.VMEM((HP, sph), F32),
            pltpu.VMEM((8, sph), F32),
            pltpu.VMEM((nby, 8, sph), F32),
            pltpu.VMEM((nbx, 8, sph), F32),
            pltpu.SemaphoreType.DMA((8,)),
            pltpu.SemaphoreType.DMA((SWEEPS, 9)),
            pltpu.SemaphoreType.DMA((SWEEPS, 9)),
            pltpu.SemaphoreType.DMA((nby,)),
            pltpu.SemaphoreType.DMA((nby,)),
            pltpu.SemaphoreType.DMA((nbx,)),
            pltpu.SemaphoreType.DMA((nbx,)),
        ],
        compiler_params=pltpu.CompilerParams(
            collective_id=0, has_side_effects=True, vmem_limit_bytes=63 * 1024 * 1024
        ),
        cost_estimate=pl.CostEstimate(
            flops=2 * SWEEPS * slots * sph * (2304 * HP + 6 * npad * HP),
            bytes_accessed=4 * 1024 * 1024,
            transcendentals=slots * sph * HP,
        ),
    )(
        psi.reshape(lh, sph),
        nbr_block.reshape(slots, sph),
        nbr_sphere.reshape(slots, sph),
        counts.reshape(1, sph),
        couple.reshape(npts, slots, sph),
        ratio.reshape(slots, sph),
        jnp.asarray(basis.astype(np.float32)),
        jnp.asarray(basis.T.astype(np.float32)),
    )
    return out.reshape(lh, 1, 1, sph), norms[:SWEEPS, 0]


def solution(mesh):
    return jax.shard_map(
        functools.partial(on_device, mesh.shape["bx"], mesh.shape["by"]),
        mesh=mesh,
        in_specs=(
            P(None, "bx", "by", "grp"),
            P("bx", "by", None, "grp"),
            P("bx", "by", None, "grp"),
            P("bx", "by", "grp"),
            P(None, "bx", "by", None, "grp"),
            P("bx", "by", None, "grp"),
        ),
        out_specs=(P(None, "bx", "by", "grp"), P("grp")),
        check_vma=False,
    )
```

```python
import functools
import math

import jax
import jax.numpy as jnp
import numpy as np
from jax import lax
from jax.experimental import pallas as pl
from jax.experimental.pallas import tpu as pltpu
from jax.sharding import PartitionSpec as P

SWEEPS = 3
MESH = pl.DeviceIdType.MESH
GOLDEN = 2.399963229728653
HP = 128
WIDE = 8
DIRECT = 32
ORDER = (4, 3, 5, 1, 7, 0, 2, 6, 8)
EARLY = 5
BF = jnp.bfloat16
F32 = jnp.float32


def basis_table(npts, lmax):
    index = np.arange(npts, dtype=np.float64)
    zval = 1.0 - (2.0 * index + 1.0) / npts
    sinval = np.sqrt(np.maximum(1.0 - zval * zval, 0.0))
    angle = GOLDEN * index
    table = {(0, 0): np.full((npts,), 1.0 / math.sqrt(4.0 * math.pi))}
    for order in range(1, lmax + 1):
        table[order, order] = (
            -math.sqrt((2.0 * order + 1.0) / (2.0 * order)) * sinval * table[order - 1, order - 1]
        )
    for order in range(0, lmax):
        table[order + 1, order] = math.sqrt(2.0 * order + 3.0) * zval * table[order, order]
    for order in range(0, lmax + 1):
        for degree in range(order + 2, lmax + 1):
            first = math.sqrt((4.0 * degree * degree - 1.0) / (degree * degree - order * order))
            second = math.sqrt(
                ((degree - 1.0) ** 2 - order * order) / (4.0 * (degree - 1.0) ** 2 - 1.0)
            )
            table[degree, order] = first * (
                zval * table[degree - 1, order] - second * table[degree - 2, order]
            )
    columns = []
    for degree in range(lmax + 1):
        for order in range(-degree, degree + 1):
            if order < 0:
                columns.append(math.sqrt(2.0) * table[degree, -order] * np.sin(-order * angle))
            elif order == 0:
                columns.append(table[degree, 0])
            else:
                columns.append(math.sqrt(2.0) * table[degree, order] * np.cos(order * angle))
    return np.stack(columns, axis=1)


def kernel(
    nbx, nby, cells,
    psi_hbm, nblk_hbm, nsph_hbm, cnt_hbm, couple_hbm, ratio_hbm, basis_hbm, basist_hbm,
    out_ref, norm_ref,
    psi_ref, nblk_ref, nsph_ref, cnt_ref, cin, ratio_ref, basis_ref, basist_ref,
    bc_ref, bt_ref, cf, cd, picked, onehot, power, land, solcat, sol0, nb, nland1, nland2,
    csem, ssem, rsem, s1, r1, s2, r2,
):
    lh, _, sph = psi_ref.shape
    npts, slots, _ = cin.shape
    npad = basis_ref.shape[0]
    groups = slots // WIDE
    wide = WIDE * sph
    ix, iy, ig = lax.axis_index("bx"), lax.axis_index("by"), lax.axis_index("grp")

    sources = (psi_hbm, nblk_hbm, nsph_hbm, cnt_hbm, ratio_hbm, basis_hbm, basist_hbm, couple_hbm)
    places = (psi_ref, nblk_ref, nsph_ref, cnt_ref, ratio_ref, basis_ref, basist_ref, cin)
    loads = [
        pltpu.make_async_copy(source, target, csem.at[i])
        for i, (source, target) in enumerate(zip(sources, places))
    ]
    for load in loads:
        load.start()

    dirs = ORDER[1:]
    inside = {}
    for d in dirs:
        tx, ty = ix + d // 3 - 1, iy + d % 3 - 1
        inside[d] = (tx >= 0) & (tx < nbx) & (ty >= 0) & (ty < nby)

    def device(d):
        return (ig, ix + d // 3 - 1, iy + d % 3 - 1)

    barrier = pltpu.get_barrier_semaphore()
    ranks = nbx * nby
    me = ix * nby + iy
    direct = ranks <= DIRECT

    def member(peer):
        return (ig, lax.div(peer, nby), lax.rem(peer, nby))

    if direct:
        for off in range(1, ranks):
            pl.semaphore_signal(
                barrier, inc=1, device_id=member(lax.rem(me + off, ranks)), device_id_type=MESH
            )
        count = ranks - 1
    else:
        count = jnp.int32(0)
        for d in dirs:
            count = count + inside[d].astype(jnp.int32)

            @pl.when(inside[d])
            def _(d=d):
                pl.semaphore_signal(barrier, inc=1, device_id=device(d), device_id_type=MESH)

        for off in range(1, nby):
            peer = lax.rem(iy + off, nby)
            far = jnp.abs(peer - iy) >= 2
            count = count + far.astype(jnp.int32)

            @pl.when(far)
            def _(peer=peer):
                pl.semaphore_signal(barrier, inc=1, device_id=(ig, ix, peer), device_id_type=MESH)

        for off in range(1, nbx):
            peer = lax.rem(ix + off, nbx)
            far = jnp.abs(peer - ix) >= 2
            count = count + far.astype(jnp.int32)

            @pl.when(far)
            def _(peer=peer):
                pl.semaphore_signal(barrier, inc=1, device_id=(ig, peer, iy), device_id_type=MESH)

    row = lax.broadcasted_iota(jnp.int32, (HP, sph), 0)
    degree = jnp.zeros((HP, sph), F32)
    for level in range(1, math.isqrt(lh)):
        degree = degree + (row >= level * level).astype(F32)
    inverse = jnp.where(row < lh, (2.0 * degree + 1.0) * (1.0 / (4.0 * math.pi)), 0.0)
    sol0[...] = jnp.zeros_like(sol0)
    loads[0].wait()
    sol0[pl.ds(0, lh), :] = psi_ref[...].reshape(lh, sph) * inverse[:lh]
    land[0, 4] = sol0[...]
    pl.semaphore_wait(barrier, count)

    def block_copy(t, d):
        return pltpu.make_async_remote_copy(
            src_ref=land.at[t, 4],
            dst_ref=land.at[t, 8 - d],
            send_sem=ssem.at[t, d],
            recv_sem=rsem.at[t, 8 - d],
            device_id=device(d),
            device_id_type=MESH,
        )

    def block_arrival(t, d):
        return pltpu.make_async_remote_copy(
            src_ref=land.at[t, 4],
            dst_ref=land.at[t, d],
            send_sem=ssem.at[t, d],
            recv_sem=rsem.at[t, d],
            device_id=device(d),
            device_id_type=MESH,
        )

    def send_all(t):
        for d in dirs:
            @pl.when(inside[d])
            def _(d=d):
                block_copy(t, d).start()

    def place(block, d):
        hi = block.astype(BF)
        lo = (block - hi.astype(F32)).astype(BF)
        solcat[pl.ds(0, HP), pl.ds(ORDER.index(d) * sph, sph)] = hi
        solcat[pl.ds(HP, HP), pl.ds(ORDER.index(d) * sph, sph)] = lo

    send_all(0)

    for load in loads[1:7]:
        load.wait()
    rows = lax.broadcasted_iota(jnp.int32, (9 * sph, sph), 0)
    position = jnp.zeros((slots, sph), jnp.int32)
    for at, d in enumerate(ORDER):
        position = jnp.where(nblk_ref[...] == d, at, position)
    nblk_ref[...] = position * sph + nsph_ref[...]

    def prepare(g, carry):
        for w in range(WIDE):
            s = g * WIDE + w
            lanes = pl.ds(w * sph, sph)
            index = nblk_ref[pl.ds(s, 1), :]
            onehot[g, :, lanes] = (rows == index).astype(F32).astype(BF)
            logr = jnp.log(ratio_ref[pl.ds(s, 1), :])
            raised = jnp.exp(degree * logr) * inverse
            power[g, :, lanes] = jnp.where(s < cnt_ref[...], raised, 0.0)
        return carry

    lax.fori_loop(0, groups, prepare, 0)

    quad = 4.0 * math.pi / npts
    for source, target, width, scale in (
        (basis_ref, bc_ref, HP, quad),
        (basist_ref, bt_ref, npad, 1.0),
    ):
        value = source[...] * scale
        hi = value.astype(BF)
        target[:, pl.ds(0, width)] = hi
        target[:, pl.ds(width, width)] = hi
        target[:, pl.ds(2 * width, width)] = (value - hi.astype(F32)).astype(BF)

    loads[7].wait()

    def widen(n, carry):
        cf[pl.ds(n * slots, slots), :] = cin[n].astype(F32)
        return carry

    lax.fori_loop(0, npts, widen, 0, unroll=2)
    cf[pl.ds(npts * slots, (npad - npts) * slots), :] = jnp.zeros(((npad - npts) * slots, sph), F32)

    def turn(g, carry):
        for w in range(WIDE):
            cd[g, :, pl.ds(w * sph, sph)] = cf[pl.ds(g * WIDE + w, npad, stride=slots), :]
        return carry

    lax.fori_loop(0, groups, turn, 0)

    def arrive(t, blocks):
        for d in blocks:
            @pl.when(inside[d])
            def _(d=d, t=t):
                block_arrival(t, d).wait_recv()
                place(land[t, d], d)

            if t == 0:
                @pl.when(jnp.logical_not(inside[d]))
                def _(d=d):
                    solcat[:, pl.ds(ORDER.index(d) * sph, sph)] = jnp.zeros((2 * HP, sph), BF)

    early = EARLY * sph

    def pick_early(g, carry):
        picked[g] = jnp.dot(
            solcat[:, pl.ds(0, early)], onehot[g, pl.ds(0, early), :], preferred_element_type=F32
        ).astype(BF)
        return carry

    def pick_late(g, carry):
        rest = jnp.dot(
            solcat[:, pl.ds(early, 9 * sph - early)],
            onehot[g, pl.ds(early, 9 * sph - early), :],
            preferred_element_type=F32,
        )
        picked[g] = (picked[g].astype(F32) + rest).astype(BF)
        return carry

    nb[...] = jnp.zeros_like(nb)
    for t in range(SWEEPS):
        old = land[t, 4]
        place(old, 4)
        arrive(t, ORDER[1:EARLY])
        lax.fori_loop(0, groups, pick_early, 0, unroll=2)
        arrive(t, ORDER[EARLY:])
        lax.fori_loop(0, groups, pick_late, 0, unroll=2)

        def pairs(g, total):
            chosen = picked[g]
            stacked = jnp.concatenate([chosen, chosen[:HP]], axis=0)
            points = jnp.dot(bc_ref[...], stacked, preferred_element_type=F32)
            product = points * cd[g]
            hi = product.astype(BF)
            lo = (product - hi.astype(F32)).astype(BF)
            back = jnp.dot(
                bt_ref[...], jnp.concatenate([hi, lo, hi], axis=0), preferred_element_type=F32
            )
            terms = back * power[g]
            for w in range(WIDE):
                total = total + terms[:, w * sph:(w + 1) * sph]
            return total

        total = lax.fori_loop(0, groups, pairs, jnp.zeros((HP, sph), F32), unroll=2)
        fresh = sol0[...] - total
        if t < SWEEPS - 1:
            land[t + 1, 4] = fresh
            send_all(t + 1)
        else:
            out_ref[...] = fresh[:lh]
        nb[pl.ds(t, 1), :] = jnp.sum((fresh - old) ** 2, axis=0, keepdims=True)

    def reduce_line(mine, slots_ref, send, recv, me, count, where):
        slots_ref[me] = mine
        copies = []
        for off in range(1, count):
            peer = lax.rem(me + off, count)
            copy = pltpu.make_async_remote_copy(
                src_ref=slots_ref.at[me],
                dst_ref=slots_ref.at[me],
                send_sem=send.at[off],
                recv_sem=recv.at[me],
                device_id=where(peer),
                device_id_type=MESH,
            )
            copy.start()
            copies.append(copy)
        for off in range(1, count):
            peer = lax.rem(me + off, count)
            pltpu.make_async_remote_copy(
                src_ref=slots_ref.at[me],
                dst_ref=slots_ref.at[peer],
                send_sem=send.at[off],
                recv_sem=recv.at[peer],
                device_id=where(peer),
                device_id_type=MESH,
            ).wait_recv()
        result = slots_ref[0]
        for i in range(1, count):
            result = result + slots_ref[i]
        for copy in copies:
            copy.wait_send()
        return result

    if direct:
        part = reduce_line(nb[...], nland1, s1, r1, me, ranks, member)
    else:
        part = reduce_line(nb[...], nland1, s1, r1, iy, nby, lambda p: (ig, ix, p))
        part = reduce_line(part, nland2, s2, r2, ix, nbx, lambda p: (ig, p, iy))
    norm = jnp.sqrt(jnp.sum(part, axis=1, keepdims=True) * (1.0 / cells))
    norm_ref[...] = jnp.broadcast_to(norm, norm_ref.shape)

    for t in range(SWEEPS):
        for d in dirs:
            @pl.when(inside[d])
            def _(d=d, t=t):
                block_copy(t, d).wait_send()


def on_device(nbx, nby, psi, nbr_block, nbr_sphere, counts, couple, ratio):
    lh, sph = psi.shape[0], psi.shape[3]
    slots = nbr_block.shape[2]
    npts = couple.shape[0]
    lmax = math.isqrt(lh) - 1
    npad = -(-npts // 16) * 16
    basis = np.zeros((npad, HP))
    basis[:npts, :lh] = basis_table(npts, lmax)
    cells = lh * sph * nbx * nby
    groups = slots // WIDE
    line = nbx * nby if nbx * nby <= DIRECT else nby
    vmem = pl.BlockSpec(memory_space=pltpu.VMEM)
    out, norms = pl.pallas_call(
        functools.partial(kernel, nbx, nby, cells),
        out_shape=(
            jax.ShapeDtypeStruct((lh, sph), F32),
            jax.ShapeDtypeStruct((8, 128), F32),
        ),
        in_specs=[pl.BlockSpec(memory_space=pltpu.HBM)] * 8,
        out_specs=(vmem, vmem),
        scratch_shapes=[
            pltpu.VMEM((lh, 1, sph), F32),
            pltpu.VMEM((slots, sph), jnp.int32),
            pltpu.VMEM((slots, sph), jnp.int32),
            pltpu.VMEM((1, sph), jnp.int32),
            pltpu.VMEM((npts, slots, sph), BF),
            pltpu.VMEM((slots, sph), F32),
            pltpu.VMEM((npad, HP), F32),
            pltpu.VMEM((HP, npad), F32),
            pltpu.VMEM((npad, 3 * HP), BF),
            pltpu.VMEM((HP, 3 * npad), BF),
            pltpu.VMEM((npad * slots, sph), F32),
            pltpu.VMEM((groups, npad, WIDE * sph), F32),
            pltpu.VMEM((groups, 2 * HP, WIDE * sph), BF),
            pltpu.VMEM((groups, 9 * sph, WIDE * sph), BF),
            pltpu.VMEM((groups, HP, WIDE * sph), F32),
            pltpu.VMEM((SWEEPS, 9, HP, sph), F32),
            pltpu.VMEM((2 * HP, 9 * sph), BF),
            pltpu.VMEM((HP, sph), F32),
            pltpu.VMEM((8, sph), F32),
            pltpu.VMEM((line, 8, sph), F32),
            pltpu.VMEM((nbx, 8, sph), F32),
            pltpu.SemaphoreType.DMA((8,)),
            pltpu.SemaphoreType.DMA((SWEEPS, 9)),
            pltpu.SemaphoreType.DMA((SWEEPS, 9)),
            pltpu.SemaphoreType.DMA((line,)),
            pltpu.SemaphoreType.DMA((line,)),
            pltpu.SemaphoreType.DMA((nbx,)),
            pltpu.SemaphoreType.DMA((nbx,)),
        ],
        compiler_params=pltpu.CompilerParams(
            collective_id=0, has_side_effects=True, vmem_limit_bytes=63 * 1024 * 1024
        ),
        cost_estimate=pl.CostEstimate(
            flops=2 * SWEEPS * slots * sph * (2304 * HP + 6 * npad * HP),
            bytes_accessed=4 * 1024 * 1024,
            transcendentals=slots * sph * HP,
        ),
    )(
        psi.reshape(lh, 1, sph),
        nbr_block.reshape(slots, sph),
        nbr_sphere.reshape(slots, sph),
        counts.reshape(1, sph),
        couple.reshape(npts, slots, sph),
        ratio.reshape(slots, sph),
        jnp.asarray(basis.astype(np.float32)),
        jnp.asarray(basis.T.astype(np.float32)),
    )
    return out.reshape(lh, 1, 1, sph), norms[:SWEEPS, 0]


def solution(mesh):
    return jax.shard_map(
        functools.partial(on_device, mesh.shape["bx"], mesh.shape["by"]),
        mesh=mesh,
        in_specs=(
            P(None, "bx", "by", "grp"),
            P("bx", "by", None, "grp"),
            P("bx", "by", None, "grp"),
            P("bx", "by", "grp"),
            P(None, "bx", "by", None, "grp"),
            P("bx", "by", None, "grp"),
        ),
        out_specs=(P(None, "bx", "by", "grp"), P("grp")),
        check_vma=False,
    )
```

```python
import functools
import math

import jax
import jax.numpy as jnp
import numpy as np
from jax import lax
from jax.experimental import pallas as pl
from jax.experimental.pallas import tpu as pltpu
from jax.sharding import PartitionSpec as P

SWEEPS = 3
MESH = pl.DeviceIdType.MESH
GOLDEN = 2.399963229728653
HP = 128
WIDE = 8
DIRECT = 32
ORDER = (4, 3, 5, 1, 7, 0, 2, 6, 8)
EARLY = 5
BF = jnp.bfloat16
F32 = jnp.float32


def basis_table(npts, lmax):
    index = np.arange(npts, dtype=np.float64)
    zval = 1.0 - (2.0 * index + 1.0) / npts
    sinval = np.sqrt(np.maximum(1.0 - zval * zval, 0.0))
    angle = GOLDEN * index
    table = {(0, 0): np.full((npts,), 1.0 / math.sqrt(4.0 * math.pi))}
    for order in range(1, lmax + 1):
        table[order, order] = (
            -math.sqrt((2.0 * order + 1.0) / (2.0 * order)) * sinval * table[order - 1, order - 1]
        )
    for order in range(0, lmax):
        table[order + 1, order] = math.sqrt(2.0 * order + 3.0) * zval * table[order, order]
    for order in range(0, lmax + 1):
        for degree in range(order + 2, lmax + 1):
            first = math.sqrt((4.0 * degree * degree - 1.0) / (degree * degree - order * order))
            second = math.sqrt(
                ((degree - 1.0) ** 2 - order * order) / (4.0 * (degree - 1.0) ** 2 - 1.0)
            )
            table[degree, order] = first * (
                zval * table[degree - 1, order] - second * table[degree - 2, order]
            )
    columns = []
    for degree in range(lmax + 1):
        for order in range(-degree, degree + 1):
            if order < 0:
                columns.append(math.sqrt(2.0) * table[degree, -order] * np.sin(-order * angle))
            elif order == 0:
                columns.append(table[degree, 0])
            else:
                columns.append(math.sqrt(2.0) * table[degree, order] * np.cos(order * angle))
    return np.stack(columns, axis=1)


def kernel(
    nbx, nby, cells,
    psi_hbm, nblk_hbm, nsph_hbm, cnt_hbm, couple_hbm, ratio_hbm, basis_hbm, basist_hbm,
    out_ref, norm_ref,
    psi_ref, nblk_ref, nsph_ref, cnt_ref, cin, ratio_ref, basis_ref, basist_ref,
    bc_ref, bt_ref, cf, cd, picked, onehot, power, land, solcat, sol0, nb, nland1, nland2,
    csem, ssem, rsem, s1, r1, s2, r2,
):
    lh, _, sph = psi_ref.shape
    npts, slots, _ = cin.shape
    npad = basis_ref.shape[0]
    groups = slots // WIDE
    wide = WIDE * sph
    ix, iy, ig = lax.axis_index("bx"), lax.axis_index("by"), lax.axis_index("grp")

    sources = (psi_hbm, nblk_hbm, nsph_hbm, cnt_hbm, ratio_hbm, basis_hbm, basist_hbm, couple_hbm)
    places = (psi_ref, nblk_ref, nsph_ref, cnt_ref, ratio_ref, basis_ref, basist_ref, cin)
    loads = [
        pltpu.make_async_copy(source, target, csem.at[i])
        for i, (source, target) in enumerate(zip(sources, places))
    ]
    for load in loads:
        load.start()

    dirs = ORDER[1:]
    inside = {}
    for d in dirs:
        tx, ty = ix + d // 3 - 1, iy + d % 3 - 1
        inside[d] = (tx >= 0) & (tx < nbx) & (ty >= 0) & (ty < nby)

    def device(d):
        return (ig, ix + d // 3 - 1, iy + d % 3 - 1)

    barrier = pltpu.get_barrier_semaphore()
    ranks = nbx * nby
    me = ix * nby + iy
    direct = ranks <= DIRECT

    def member(peer):
        return (ig, lax.div(peer, nby), lax.rem(peer, nby))

    if direct:
        for off in range(1, ranks):
            pl.semaphore_signal(
                barrier, inc=1, device_id=member(lax.rem(me + off, ranks)), device_id_type=MESH
            )
        count = ranks - 1
    else:
        count = jnp.int32(0)
        for d in dirs:
            count = count + inside[d].astype(jnp.int32)

            @pl.when(inside[d])
            def _(d=d):
                pl.semaphore_signal(barrier, inc=1, device_id=device(d), device_id_type=MESH)

        for off in range(1, nby):
            peer = lax.rem(iy + off, nby)
            far = jnp.abs(peer - iy) >= 2
            count = count + far.astype(jnp.int32)

            @pl.when(far)
            def _(peer=peer):
                pl.semaphore_signal(barrier, inc=1, device_id=(ig, ix, peer), device_id_type=MESH)

        for off in range(1, nbx):
            peer = lax.rem(ix + off, nbx)
            far = jnp.abs(peer - ix) >= 2
            count = count + far.astype(jnp.int32)

            @pl.when(far)
            def _(peer=peer):
                pl.semaphore_signal(barrier, inc=1, device_id=(ig, peer, iy), device_id_type=MESH)

    row = lax.broadcasted_iota(jnp.int32, (HP, sph), 0)
    degree = jnp.zeros((HP, sph), F32)
    for level in range(1, math.isqrt(lh)):
        degree = degree + (row >= level * level).astype(F32)
    inverse = jnp.where(row < lh, (2.0 * degree + 1.0) * (1.0 / (4.0 * math.pi)), 0.0)
    sol0[...] = jnp.zeros_like(sol0)
    loads[0].wait()
    sol0[pl.ds(0, lh), :] = psi_ref[...].reshape(lh, sph) * inverse[:lh]
    land[0, 4] = sol0[...]
    pl.semaphore_wait(barrier, count)

    def block_copy(t, d):
        return pltpu.make_async_remote_copy(
            src_ref=land.at[t, 4],
            dst_ref=land.at[t, 8 - d],
            send_sem=ssem.at[t, d],
            recv_sem=rsem.at[t, 8 - d],
            device_id=device(d),
            device_id_type=MESH,
        )

    def block_arrival(t, d):
        return pltpu.make_async_remote_copy(
            src_ref=land.at[t, 4],
            dst_ref=land.at[t, d],
            send_sem=ssem.at[t, d],
            recv_sem=rsem.at[t, d],
            device_id=device(d),
            device_id_type=MESH,
        )

    def send_all(t):
        for d in dirs:
            @pl.when(inside[d])
            def _(d=d):
                block_copy(t, d).start()

    def place(block, d):
        hi = block.astype(BF)
        lo = (block - hi.astype(F32)).astype(BF)
        solcat[pl.ds(0, HP), pl.ds(ORDER.index(d) * sph, sph)] = hi
        solcat[pl.ds(HP, HP), pl.ds(ORDER.index(d) * sph, sph)] = lo

    send_all(0)

    for load in loads[1:7]:
        load.wait()
    rows = lax.broadcasted_iota(jnp.int32, (9 * sph, sph), 0)
    position = jnp.zeros((slots, sph), jnp.int32)
    for at, d in enumerate(ORDER):
        position = jnp.where(nblk_ref[...] == d, at, position)
    nblk_ref[...] = position * sph + nsph_ref[...]

    def prepare(g, carry):
        for w in range(WIDE):
            s = g * WIDE + w
            lanes = pl.ds(w * sph, sph)
            index = nblk_ref[pl.ds(s, 1), :]
            onehot[g, :, lanes] = (rows == index).astype(F32).astype(BF)
            logr = jnp.log(ratio_ref[pl.ds(s, 1), :])
            raised = jnp.exp(degree * logr) * inverse
            power[g, :, lanes] = jnp.where(s < cnt_ref[...], raised, 0.0)
        return carry

    lax.fori_loop(0, groups, prepare, 0)

    quad = 4.0 * math.pi / npts
    for source, target, width, scale in (
        (basis_ref, bc_ref, HP, quad),
        (basist_ref, bt_ref, npad, 1.0),
    ):
        value = source[...] * scale
        hi = value.astype(BF)
        target[:, pl.ds(0, width)] = hi
        target[:, pl.ds(width, width)] = hi
        target[:, pl.ds(2 * width, width)] = (value - hi.astype(F32)).astype(BF)

    loads[7].wait()

    def widen(n, carry):
        cf[pl.ds(n * slots, slots), :] = cin[n].astype(F32)
        return carry

    lax.fori_loop(0, npts, widen, 0, unroll=2)
    cf[pl.ds(npts * slots, (npad - npts) * slots), :] = jnp.zeros(((npad - npts) * slots, sph), F32)

    def turn(g, carry):
        for w in range(WIDE):
            cd[g, :, pl.ds(w * sph, sph)] = cf[pl.ds(g * WIDE + w, npad, stride=slots), :]
        return carry

    lax.fori_loop(0, groups, turn, 0)

    def arrive(t, blocks):
        for d in blocks:
            @pl.when(inside[d])
            def _(d=d, t=t):
                block_arrival(t, d).wait_recv()
                place(land[t, d], d)

            if t == 0:
                @pl.when(jnp.logical_not(inside[d]))
                def _(d=d):
                    solcat[:, pl.ds(ORDER.index(d) * sph, sph)] = jnp.zeros((2 * HP, sph), BF)

    early = EARLY * sph

    def pick_early(g, carry):
        picked[g] = jnp.dot(
            solcat[:, pl.ds(0, early)], onehot[g, pl.ds(0, early), :], preferred_element_type=F32
        ).astype(BF)
        return carry

    def pick_late(g, carry):
        rest = jnp.dot(
            solcat[:, pl.ds(early, 9 * sph - early)],
            onehot[g, pl.ds(early, 9 * sph - early), :],
            preferred_element_type=F32,
        )
        picked[g] = (picked[g].astype(F32) + rest).astype(BF)
        return carry

    nb[...] = jnp.zeros_like(nb)
    for t in range(SWEEPS):
        old = land[t, 4]
        place(old, 4)
        arrive(t, ORDER[1:EARLY])
        lax.fori_loop(0, groups, pick_early, 0, unroll=2)
        arrive(t, ORDER[EARLY:])
        lax.fori_loop(0, groups, pick_late, 0, unroll=2)

        def pairs(g, total):
            chosen = picked[g]
            stacked = jnp.concatenate([chosen, chosen[:HP]], axis=0)
            points = jnp.dot(bc_ref[...], stacked, preferred_element_type=F32)
            product = points * cd[g]
            hi = product.astype(BF)
            lo = (product - hi.astype(F32)).astype(BF)
            back = jnp.dot(
                bt_ref[...], jnp.concatenate([hi, lo, hi], axis=0), preferred_element_type=F32
            )
            terms = back * power[g]
            for w in range(WIDE):
                total = total + terms[:, w * sph:(w + 1) * sph]
            return total

        total = lax.fori_loop(0, groups, pairs, jnp.zeros((HP, sph), F32), unroll=4)
        fresh = sol0[...] - total
        if t < SWEEPS - 1:
            land[t + 1, 4] = fresh
            send_all(t + 1)
        else:
            out_ref[...] = fresh[:lh]
        nb[pl.ds(t, 1), :] = jnp.sum((fresh - old) ** 2, axis=0, keepdims=True)

    def reduce_line(mine, slots_ref, send, recv, me, count, where):
        slots_ref[me] = mine
        copies = []
        for off in range(1, count):
            peer = lax.rem(me + off, count)
            copy = pltpu.make_async_remote_copy(
                src_ref=slots_ref.at[me],
                dst_ref=slots_ref.at[me],
                send_sem=send.at[off],
                recv_sem=recv.at[me],
                device_id=where(peer),
                device_id_type=MESH,
            )
            copy.start()
            copies.append(copy)
        for off in range(1, count):
            peer = lax.rem(me + off, count)
            pltpu.make_async_remote_copy(
                src_ref=slots_ref.at[me],
                dst_ref=slots_ref.at[peer],
                send_sem=send.at[off],
                recv_sem=recv.at[peer],
                device_id=where(peer),
                device_id_type=MESH,
            ).wait_recv()
        result = slots_ref[0]
        for i in range(1, count):
            result = result + slots_ref[i]
        for copy in copies:
            copy.wait_send()
        return result

    if direct:
        part = reduce_line(nb[...], nland1, s1, r1, me, ranks, member)
    else:
        part = reduce_line(nb[...], nland1, s1, r1, iy, nby, lambda p: (ig, ix, p))
        part = reduce_line(part, nland2, s2, r2, ix, nbx, lambda p: (ig, p, iy))
    norm = jnp.sqrt(jnp.sum(part, axis=1, keepdims=True) * (1.0 / cells))
    norm_ref[...] = jnp.broadcast_to(norm, norm_ref.shape)

    for t in range(SWEEPS):
        for d in dirs:
            @pl.when(inside[d])
            def _(d=d, t=t):
                block_copy(t, d).wait_send()


def on_device(nbx, nby, psi, nbr_block, nbr_sphere, counts, couple, ratio):
    lh, sph = psi.shape[0], psi.shape[3]
    slots = nbr_block.shape[2]
    npts = couple.shape[0]
    lmax = math.isqrt(lh) - 1
    npad = -(-npts // 16) * 16
    basis = np.zeros((npad, HP))
    basis[:npts, :lh] = basis_table(npts, lmax)
    cells = lh * sph * nbx * nby
    groups = slots // WIDE
    line = nbx * nby if nbx * nby <= DIRECT else nby
    vmem = pl.BlockSpec(memory_space=pltpu.VMEM)
    out, norms = pl.pallas_call(
        functools.partial(kernel, nbx, nby, cells),
        out_shape=(
            jax.ShapeDtypeStruct((lh, sph), F32),
            jax.ShapeDtypeStruct((8, 128), F32),
        ),
        in_specs=[pl.BlockSpec(memory_space=pltpu.HBM)] * 8,
        out_specs=(vmem, vmem),
        scratch_shapes=[
            pltpu.VMEM((lh, 1, sph), F32),
            pltpu.VMEM((slots, sph), jnp.int32),
            pltpu.VMEM((slots, sph), jnp.int32),
            pltpu.VMEM((1, sph), jnp.int32),
            pltpu.VMEM((npts, slots, sph), BF),
            pltpu.VMEM((slots, sph), F32),
            pltpu.VMEM((npad, HP), F32),
            pltpu.VMEM((HP, npad), F32),
            pltpu.VMEM((npad, 3 * HP), BF),
            pltpu.VMEM((HP, 3 * npad), BF),
            pltpu.VMEM((npad * slots, sph), F32),
            pltpu.VMEM((groups, npad, WIDE * sph), F32),
            pltpu.VMEM((groups, 2 * HP, WIDE * sph), BF),
            pltpu.VMEM((groups, 9 * sph, WIDE * sph), BF),
            pltpu.VMEM((groups, HP, WIDE * sph), F32),
            pltpu.VMEM((SWEEPS, 9, HP, sph), F32),
            pltpu.VMEM((2 * HP, 9 * sph), BF),
            pltpu.VMEM((HP, sph), F32),
            pltpu.VMEM((8, sph), F32),
            pltpu.VMEM((line, 8, sph), F32),
            pltpu.VMEM((nbx, 8, sph), F32),
            pltpu.SemaphoreType.DMA((8,)),
            pltpu.SemaphoreType.DMA((SWEEPS, 9)),
            pltpu.SemaphoreType.DMA((SWEEPS, 9)),
            pltpu.SemaphoreType.DMA((line,)),
            pltpu.SemaphoreType.DMA((line,)),
            pltpu.SemaphoreType.DMA((nbx,)),
            pltpu.SemaphoreType.DMA((nbx,)),
        ],
        compiler_params=pltpu.CompilerParams(
            collective_id=0, has_side_effects=True, vmem_limit_bytes=63 * 1024 * 1024
        ),
        cost_estimate=pl.CostEstimate(
            flops=2 * SWEEPS * slots * sph * (2304 * HP + 6 * npad * HP),
            bytes_accessed=4 * 1024 * 1024,
            transcendentals=slots * sph * HP,
        ),
    )(
        psi.reshape(lh, 1, sph),
        nbr_block.reshape(slots, sph),
        nbr_sphere.reshape(slots, sph),
        counts.reshape(1, sph),
        couple.reshape(npts, slots, sph),
        ratio.reshape(slots, sph),
        jnp.asarray(basis.astype(np.float32)),
        jnp.asarray(basis.T.astype(np.float32)),
    )
    return out.reshape(lh, 1, 1, sph), norms[:SWEEPS, 0]


def solution(mesh):
    return jax.shard_map(
        functools.partial(on_device, mesh.shape["bx"], mesh.shape["by"]),
        mesh=mesh,
        in_specs=(
            P(None, "bx", "by", "grp"),
            P("bx", "by", None, "grp"),
            P("bx", "by", None, "grp"),
            P("bx", "by", "grp"),
            P(None, "bx", "by", None, "grp"),
            P("bx", "by", None, "grp"),
        ),
        out_specs=(P(None, "bx", "by", "grp"), P("grp")),
        check_vma=False,
    )
```
